32 devices in a mesh: grp: 4 (over y, x), dev: 8 (over z, core).
Axes of the slice: x: 2, y: 2, z: 4, core: 2. Of those that a mesh axis runs over, the one named last changes fastest.
Arguments:
- embedding: bfloat16 [32768, 256], P(('grp', 'dev')), may hold values from -6 to 6
- cotangent: bfloat16 [32768, 256], P(('grp', 'dev')), may hold values from -6 to 6
- fractional: bfloat16 [3, 32768], P(None, ('grp', 'dev')), may hold values from 0 to 1
- wave_index: int32 [3, 512], replicated, may hold values from -8 to 8
- tile_pairs: int32 [768, 2], P(('grp', 'dev')), may hold values from 0 to 15, as said below
- counts: int32 [32], P(('grp', 'dev')), may hold values from 3 to 24, as said below
- wave_filter: float32 [512, 256], replicated, may hold values from -0.25 to 0.25
- short_weight: bfloat16 [256, 256], replicated, may hold values from -0.375 to 0.375
Outputs:
- message: bfloat16 [32768, 256], P(('grp', 'dev'))
- embedding_grad: bfloat16 [32768, 256], P(('grp', 'dev'))
The draws below stay inside these ranges and needn't reach their ends.
Inputs may be any that keep to these rules, and one draw needn't show every extreme that they name: `tile_pairs`: in each block's 24 rows, column 0 is one of the block's 8 tiles and column 1 one of 16 tiles: the block's own, then the next block's. The first row of every block names a tile of the next block. `counts`: some block has exactly 24 live rows in every draw.
All inputs are finite; a program needn't handle non-finite values.
Results may differ from the reference program's by a relative error of at most 0.0059.
Values may be sent and summed in bfloat16 or wider, within the bound.
A program may use at most 64 MiB of HBM per device.

```python
import math
import jax
import jax.numpy as jnp
from jax import lax

C = 256
K = 512
TILE = 128
ATOM_DEV = 1024
PAIRS_MAX = 24
BLOCKS = 32
ATOMS = 32768


def draw_tile_pairs(key, part):
    tiles = ATOM_DEV // TILE
    firsts = jax.random.randint(jax.random.fold_in(key, 21), (BLOCKS * PAIRS_MAX,), 0, tiles)
    seconds = jax.random.randint(jax.random.fold_in(key, 22), (BLOCKS * PAIRS_MAX,), 0, 2 * tiles)
    reaching = tiles + jax.random.randint(jax.random.fold_in(key, 23), (BLOCKS * PAIRS_MAX,), 0, tiles)
    rows = jnp.arange(BLOCKS * PAIRS_MAX, dtype=jnp.int32)
    seconds = jnp.where(rows % PAIRS_MAX == 0, reaching, seconds)
    seconds = jnp.where(rows == 0, 2 * tiles - 1, seconds)
    seconds = jnp.where(rows == 1, 0, seconds)
    firsts = jnp.where(rows == 1, 0, firsts)
    return jnp.stack([firsts, seconds], axis=1).astype(jnp.int32)


def draw_counts(key, part):
    levels = jax.random.randint(jax.random.fold_in(key, 31), (BLOCKS,), 0, 4)
    powers = jnp.left_shift(jnp.ones((BLOCKS,), jnp.int32), levels.astype(jnp.int32))
    shares = (PAIRS_MAX + powers - 1) // powers
    busiest = jax.random.randint(jax.random.fold_in(key, 32), (), 0, BLOCKS)
    return jnp.where(jnp.arange(BLOCKS) == busiest, PAIRS_MAX, shares).astype(jnp.int32)


def with_ends(result, rng, low, high):
    longest = result.shape.index(max(result.shape))
    spots = []
    for shift in (0, 1):
        where = [jax.random.randint(jax.random.fold_in(rng, axis), (), 0, length) for axis, length in enumerate(result.shape)]
        where[longest] = (where[longest] + shift) % result.shape[longest]
        spots.append(tuple(where))
    return result.at[spots[0]].set(low).at[spots[1]].set(high)


def steps_of(stream_key, shape, cuts, smallest, largest):
    loudness, own = 1.0, jax.random.fold_in(stream_key, 6)
    for dim, parts in cuts:
        draws = jnp.exp(jax.random.uniform(jax.random.fold_in(own, dim), (parts,), jnp.float32, smallest / len(cuts), largest / len(cuts)))
        loudness = loudness * jnp.repeat(draws, shape[dim] // parts).reshape([-1 if axis == dim else 1 for axis in range(len(shape))])
    return loudness


def noise(own_key, shape, deviation, reach, shards=(), kind=jnp.bfloat16):
    array = deviation * jax.random.normal(own_key, shape, jnp.float32)
    if shards:
        array = array * steps_of(own_key, shape, shards, -0.22, 0.18)
    return jnp.clip(array, -reach, reach).astype(kind)


def setup_inputs(seed: int = 0) -> dict:
    streams_of = jax.random.split(jax.random.key(seed), 9)
    return {
        "embedding": noise(streams_of[0], (ATOMS, C), 1.0, 6.0, ((0, 32),)),
        "cotangent": noise(streams_of[1], (ATOMS, C), 1.0, 6.0, ((0, 32),)),
        "fractional": jnp.clip(1.0 * jax.random.uniform(streams_of[2], (3, ATOMS), jnp.float32) ** steps_of(streams_of[2], (3, ATOMS), ((1, 32),), -0.2, 0.2), 0.0, 1.0).astype(jnp.bfloat16),
        "wave_index": with_ends(jax.random.randint(streams_of[3], (3, K), -8, 9), jax.random.fold_in(streams_of[3], 1), -8, 8).astype(jnp.int32),
        "tile_pairs": draw_tile_pairs(jax.random.fold_in(streams_of[8], 71), 0),
        "counts": draw_counts(jax.random.fold_in(streams_of[8], 71), 0),
        "wave_filter": noise(streams_of[6], (K, C), K ** -0.5, 0.25, (), jnp.float32),
        "short_weight": noise(streams_of[7], (C, C), C ** -0.5, 0.375),
    }


two_pi = 2.0 * math.pi

def trig_table(places, wave_index):
    phase = two_pi * jnp.dot(places.astype(jnp.float32).T, wave_index.astype(jnp.float32), precision=lax.Precision.HIGHEST)
    return jnp.concatenate([jnp.cos(phase), jnp.sin(phase)], axis=1).astype(jnp.bfloat16)

def pair_kernel(left_places, right_places):
    left = left_places.astype(jnp.float32)
    right = right_places.astype(jnp.float32)
    wave = jnp.sin(math.pi * (left[:, :, None] - right[:, None, :]))
    spread = jnp.exp(-2.0 * lax.optimization_barrier(jnp.sum(wave * wave, axis=0)))
    return (spread / math.sqrt(left.shape[1])).astype(jnp.bfloat16)

def reference(embedding, cotangent, fractional, wave_index, tile_pairs, counts, wave_filter, short_weight):
    channels = embedding.shape[1]
    tile_count = ATOM_DEV // TILE
    inv_root = 1.0 / math.sqrt(ATOMS)
    place_blocks = fractional.reshape(3, BLOCKS, ATOM_DEV).transpose(1, 0, 2)
    embed_blocks = embedding.reshape(BLOCKS, ATOM_DEV, channels)
    cot_blocks = cotangent.reshape(BLOCKS, ATOM_DEV, channels)

    def add_block(total, items):
        places, embed_rows, cot_rows = items
        table = trig_table(places, wave_index)
        dims = (((0,), (0,)), ((), ()))
        first_half = lax.dot_general(table, embed_rows, dims, preferred_element_type=jnp.float32)
        second_half = lax.dot_general(table, cot_rows, dims, preferred_element_type=jnp.float32)
        return (total + jnp.concatenate([first_half, second_half], axis=1), None)
    summed, _unused = lax.scan(add_block, jnp.zeros((2 * K, 2 * channels), jnp.float32), (place_blocks, embed_blocks, cot_blocks))
    doubled = jnp.concatenate([wave_filter, wave_filter], axis=0)
    tiled = jnp.concatenate([doubled, doubled], axis=1)
    coeffs = (summed * tiled * inv_root).astype(jnp.bfloat16)
    projected = jnp.dot(embedding, short_weight, preferred_element_type=jnp.float32).astype(jnp.bfloat16)
    proj_tiles = projected.reshape(BLOCKS, tile_count, TILE, channels)
    place_tiles = fractional.reshape(3, BLOCKS, tile_count, TILE).transpose(1, 2, 0, 3)
    cot_tiles = cotangent.reshape(BLOCKS, tile_count, TILE, channels)
    pair_blocks = tile_pairs.reshape(BLOCKS, PAIRS_MAX, 2)

    def near_block(index):
        after = (index + 1) % BLOCKS
        places = jnp.concatenate([place_tiles[index], place_tiles[after]], axis=0)
        sources = jnp.concatenate([proj_tiles[index], proj_tiles[after]], axis=0)
        targets = cot_tiles[index]
        pairs = pair_blocks[index]
        firsts = pairs[:, 0].astype(jnp.int32)
        seconds = pairs[:, 1].astype(jnp.int32)
        kernels = jax.vmap(pair_kernel)(places[firsts], places[seconds]).astype(jnp.float32)
        live = (jnp.arange(PAIRS_MAX, dtype=jnp.int32) < counts[index])[:, None, None]
        ahead = jnp.einsum('pij,pjc->pic', kernels, sources[seconds].astype(jnp.float32))
        behind = jnp.einsum('pij,pic->pjc', kernels, targets[firsts].astype(jnp.float32))
        forward = jax.ops.segment_sum(jnp.where(live, ahead, 0.0), firsts, num_segments=tile_count)
        backward = jax.ops.segment_sum(jnp.where(live, behind, 0.0), seconds, num_segments=2 * tile_count)
        return (forward, backward)
    start_carry = near_block(jnp.int32(BLOCKS - 1))[1][tile_count:]

    def block_outputs(carry, index):
        forward, backward = near_block(index)
        table = trig_table(place_blocks[index], wave_index)
        long_range = jnp.dot(table, coeffs, preferred_element_type=jnp.float32)
        message = (long_range[:, :channels] + forward.reshape(ATOM_DEV, channels)).astype(jnp.bfloat16)
        near_grad = (backward[:tile_count] + carry).reshape(ATOM_DEV, channels).astype(jnp.bfloat16)
        mixed = lax.dot_general(near_grad, short_weight, (((1,), (1,)), ((), ())), preferred_element_type=jnp.float32)
        gradient = (long_range[:, channels:] + mixed).astype(jnp.bfloat16)
        return (backward[tile_count:], (message, gradient))
    _unused, outputs = lax.scan(block_outputs, start_carry, jnp.arange(BLOCKS, dtype=jnp.int32))
    message, gradient = outputs
    return (message.reshape(ATOMS, channels), gradient.reshape(ATOMS, channels))
```

```python
import math

import jax
import jax.numpy as jnp
from jax import lax
from jax.sharding import PartitionSpec as P

TILE = 128
two_pi = 2.0 * math.pi


def shifted(value, axis, by):
    size = lax.axis_size(axis)
    return lax.ppermute(value, axis, [(i, (i + by) % size) for i in range(size)])


def cos_sin(turns):
    rest = turns - jnp.round(turns)
    angle = rest * (two_pi / 4.0)
    sq = angle * angle
    sine = angle * (1.0 + sq * (-1.0 / 6 + sq * (1.0 / 120 + sq * (-1.0 / 5040 + sq * (1.0 / 362880)))))
    cosine = 1.0 + sq * (-0.5 + sq * (1.0 / 24 + sq * (-1.0 / 720 + sq * (1.0 / 40320))))
    for _ in range(2):
        sine, cosine = 2.0 * sine * cosine, 1.0 - 2.0 * sine * sine
    return cosine, sine


def trig_table(places, wave_index):
    turns = lax.dot_general(
        places, wave_index.astype(jnp.bfloat16), (((0,), (0,)), ((), ())), preferred_element_type=jnp.float32
    )
    cosine, sine = cos_sin(turns)
    return jnp.concatenate([cosine.astype(jnp.bfloat16), sine.astype(jnp.bfloat16)], axis=1)


def body(embedding, cotangent, fractional, wave_index, tile_pairs, counts, wave_filter, short_weight):
    atom_rows, channels = embedding.shape
    wave_count = wave_index.shape[1]
    tiles = atom_rows // TILE
    pair_rows = tile_pairs.shape[0]
    blocks = lax.axis_size("grp") * lax.axis_size("dev")
    inv_root = 1.0 / math.sqrt(atom_rows * blocks)
    above_embedding, above_places = shifted((embedding, fractional), ("grp", "dev"), -1)
    table = trig_table(fractional, wave_index)
    joined = jnp.concatenate([embedding, cotangent], axis=1)
    rows = 2 * wave_count // lax.axis_size("dev")
    within = lax.psum_scatter(
        lax.dot_general(table, joined, (((0,), (0,)), ((), ())), preferred_element_type=jnp.float32),
        "dev", scatter_dimension=0, tiled=True,
    )
    summed = lax.psum(within, "grp")
    local = lax.dynamic_slice_in_dim(wave_filter, lax.axis_index("dev") * rows % wave_count, rows, 0)
    coeffs = (summed * jnp.concatenate([local, local], axis=1) * inv_root).astype(jnp.bfloat16)
    coeffs = lax.all_gather(coeffs, "dev", axis=0, tiled=True)

    sources = jnp.dot(
        jnp.concatenate([embedding, above_embedding], axis=0), short_weight, preferred_element_type=jnp.float32
    ).astype(jnp.bfloat16)
    cosine, sine = cos_sin(jnp.concatenate([fractional, above_places], axis=1).astype(jnp.float32))
    waves = jnp.concatenate([cosine, sine], axis=0)
    closeness = lax.dot_general(
        waves[:, :atom_rows], waves, (((0,), (0,)), ((), ())), precision=lax.Precision.HIGHEST
    )
    live = (jnp.arange(pair_rows, dtype=jnp.int32) < counts[0])[:, None]
    first_hot = ((tile_pairs[:, :1] == jnp.arange(tiles, dtype=jnp.int32)) & live).astype(jnp.float32)
    second_hot = (tile_pairs[:, 1:] == jnp.arange(2 * tiles, dtype=jnp.int32)).astype(jnp.float32)
    times = jnp.einsum("pu,pv->uv", first_hot, second_hot)
    spread = (jnp.exp(closeness - 3.0) * (1.0 / math.sqrt(TILE))).astype(jnp.bfloat16)
    times = jnp.repeat(jnp.repeat(times, TILE, axis=0), TILE, axis=1).astype(jnp.bfloat16)
    weights = spread * times
    forward = jnp.dot(weights, sources, preferred_element_type=jnp.float32)
    backward = lax.dot_general(weights, cotangent, (((0,), (0,)), ((), ())), preferred_element_type=jnp.float32)
    below = shifted(backward[atom_rows:].astype(jnp.bfloat16), ("grp", "dev"), 1).astype(jnp.float32)
    near_grad = (backward[:atom_rows] + below).astype(jnp.bfloat16)
    mixed = lax.dot_general(near_grad, short_weight, (((1,), (1,)), ((), ())), preferred_element_type=jnp.float32)
    long_range = jnp.dot(table, coeffs, preferred_element_type=jnp.float32)
    message = (long_range[:, :channels] + forward).astype(jnp.bfloat16)
    embedding_grad = (long_range[:, channels:] + mixed).astype(jnp.bfloat16)
    return (message, embedding_grad)


def solution(mesh):
    split = P(("grp", "dev"), None)
    in_specs = (split, split, P(None, ("grp", "dev")), P(), split, P(("grp", "dev")), P(), P())
    return jax.shard_map(body, mesh=mesh, in_specs=in_specs, out_specs=(split, split), check_vma=False)
```

```python
import functools
import math

import jax
import jax.numpy as jnp
from jax import lax
from jax.experimental import pallas as pl
from jax.experimental.pallas import tpu as pltpu
from jax.sharding import PartitionSpec as P

TILE = 128
two_pi = 2.0 * math.pi


def shifted(value, axis, by):
    size = lax.axis_size(axis)
    return lax.ppermute(value, axis, [(i, (i + by) % size) for i in range(size)])


def cos_sin(turns):
    rest = turns - jnp.round(turns)
    angle = rest * (two_pi / 4.0)
    sq = angle * angle
    sine = angle * (1.0 + sq * (-1.0 / 6 + sq * (1.0 / 120 + sq * (-1.0 / 5040 + sq * (1.0 / 362880)))))
    cosine = 1.0 + sq * (-0.5 + sq * (1.0 / 24 + sq * (-1.0 / 720 + sq * (1.0 / 40320))))
    for _ in range(2):
        sine, cosine = 2.0 * sine * cosine, 1.0 - 2.0 * sine * sine
    return cosine, sine


def trig_table(places, wave_index):
    turns = lax.dot_general(
        places, wave_index.astype(jnp.bfloat16), (((0,), (0,)), ((), ())), preferred_element_type=jnp.float32
    )
    cosine, sine = cos_sin(turns)
    return jnp.concatenate([cosine.astype(jnp.bfloat16), sine.astype(jnp.bfloat16)], axis=1)


def reduce_kernel(groups, depth, inv_root, part_ref, filter_ref, out_ref, half_in, half_sum, group_in, group_sum, depth_in, send_sem, recv_sem):
    grp, dev = lax.axis_index("grp"), lax.axis_index("dev")
    place, core = dev // 2, dev % 2
    half = part_ref.shape[0] // 2
    rows = half // groups
    share = rows // depth
    scatter = rows % depth == 0 and share % 16 == 0
    other = {"dev": place * 2 + 1 - core}
    group_peers = [lax.rem(grp + s, groups) for s in range(1, groups)]
    place_peers = [lax.rem(place + s, depth) for s in range(1, depth)]
    group_ids = [{"grp": p} for p in group_peers]
    place_ids = [{"dev": p * 2 + core} for p in place_peers]
    used = [0]

    barrier = pltpu.get_barrier_semaphore()
    for who in [other, *group_ids, *place_ids]:
        pl.semaphore_signal(barrier, inc=1, device_id=who, device_id_type=pl.DeviceIdType.MESH)
    pl.semaphore_wait(barrier, 1 + len(group_ids) + len(place_ids))

    def span(start, size):
        return pl.ds(pl.multiple_of(start, 16), size)

    def exchange(moves):
        copies = []
        for source, target, who in moves:
            copies.append(pltpu.make_async_remote_copy(
                src_ref=source, dst_ref=target, send_sem=send_sem.at[used[0]], recv_sem=recv_sem.at[used[0]],
                device_id=who, device_id_type=pl.DeviceIdType.MESH,
            ))
            used[0] += 1
        for copy in copies:
            copy.start()
        for copy in copies:
            copy.wait()

    def filtered(total, start):
        gain = filter_ref[span(start, total.shape[0]), :]
        return (total * jnp.concatenate([gain, gain], axis=1) * inv_root).astype(jnp.bfloat16)

    exchange([(part_ref.at[span((1 - core) * half, half)], half_in, other)])
    half_sum[...] = (
        part_ref[span(core * half, half), :].astype(jnp.float32) + half_in[...].astype(jnp.float32)
    ).astype(jnp.bfloat16)

    exchange([
        (half_sum.at[span(p * rows, rows)], group_in.at[s], who)
        for s, (p, who) in enumerate(zip(group_peers, group_ids))
    ])
    total = half_sum[span(grp * rows, rows), :].astype(jnp.float32)
    for s in range(groups - 1):
        total = total + group_in[s].astype(jnp.float32)
    group_sum[...] = total.astype(jnp.bfloat16)

    base = core * half + grp * rows
    if scatter:
        exchange([
            (group_sum.at[span(p * share, share)], depth_in.at[s], who)
            for s, (p, who) in enumerate(zip(place_peers, place_ids))
        ])
        total = group_sum[span(place * share, share), :].astype(jnp.float32)
        for s in range(depth - 1):
            total = total + depth_in[s].astype(jnp.float32)
        mine = span(base + place * share, share)
        out_ref[mine, :] = filtered(total, grp * rows + place * share)
        exchange([(out_ref.at[mine], out_ref.at[mine], who) for who in place_ids])
    else:
        exchange([(group_sum, depth_in.at[s], who) for s, who in enumerate(place_ids)])
        total = group_sum[...].astype(jnp.float32)
        for s in range(depth - 1):
            total = total + depth_in[s].astype(jnp.float32)
        out_ref[span(base, rows), :] = filtered(total, grp * rows)
    mine = span(base, rows)
    exchange([(out_ref.at[mine], out_ref.at[mine], who) for who in group_ids])
    mine = span(core * half, half)
    exchange([(out_ref.at[mine], out_ref.at[mine], other)])


def reduced(part, wave_filter, inv_root):
    groups, depth = lax.axis_size("grp"), lax.axis_size("dev") // 2
    total_rows, width = part.shape
    half = total_rows // 2
    rows = half // groups
    share = rows // depth if rows % depth == 0 and (rows // depth) % 16 == 0 else rows
    copies = 2 + 2 * (groups - 1) + 2 * (depth - 1)
    return pl.pallas_call(
        functools.partial(reduce_kernel, groups, depth, inv_root),
        out_shape=jax.ShapeDtypeStruct(part.shape, jnp.bfloat16),
        in_specs=[pl.BlockSpec(memory_space=pltpu.VMEM)] * 2,
        out_specs=pl.BlockSpec(memory_space=pltpu.VMEM),
        scratch_shapes=[
            pltpu.VMEM((half, width), jnp.bfloat16),
            pltpu.VMEM((half, width), jnp.bfloat16),
            pltpu.VMEM((groups - 1, rows, width), jnp.bfloat16),
            pltpu.VMEM((rows, width), jnp.bfloat16),
            pltpu.VMEM((depth - 1, share, width), jnp.bfloat16),
            pltpu.SemaphoreType.DMA((copies,)),
            pltpu.SemaphoreType.DMA((copies,)),
        ],
        compiler_params=pltpu.CompilerParams(collective_id=0, has_side_effects=True, vmem_limit_bytes=16 * 2**20),
        cost_estimate=pl.CostEstimate(flops=4 * part.size, bytes_accessed=8 * part.size, transcendentals=0),
    )(part, wave_filter)


def body(embedding, cotangent, fractional, wave_index, tile_pairs, counts, wave_filter, short_weight):
    atom_rows, channels = embedding.shape
    tiles = atom_rows // TILE
    pair_rows = tile_pairs.shape[0]
    blocks = lax.axis_size("grp") * lax.axis_size("dev")
    inv_root = 1.0 / math.sqrt(atom_rows * blocks)
    above_embedding, above_places = shifted((embedding, fractional), ("grp", "dev"), -1)
    table = trig_table(fractional, wave_index)
    joined = jnp.concatenate([embedding, cotangent], axis=1)
    part = lax.dot_general(table, joined, (((0,), (0,)), ((), ())), preferred_element_type=jnp.float32)
    coeffs = reduced(part.astype(jnp.bfloat16), wave_filter, inv_root)

    sources = jnp.dot(
        jnp.concatenate([embedding, above_embedding], axis=0), short_weight, preferred_element_type=jnp.float32
    ).astype(jnp.bfloat16)
    cosine, sine = cos_sin(jnp.concatenate([fractional, above_places], axis=1).astype(jnp.float32))
    waves = jnp.concatenate([cosine, sine], axis=0)
    closeness = lax.dot_general(
        waves[:, :atom_rows], waves, (((0,), (0,)), ((), ())), precision=lax.Precision.HIGHEST
    )
    live = (jnp.arange(pair_rows, dtype=jnp.int32) < counts[0])[:, None]
    first_hot = ((tile_pairs[:, :1] == jnp.arange(tiles, dtype=jnp.int32)) & live).astype(jnp.float32)
    second_hot = (tile_pairs[:, 1:] == jnp.arange(2 * tiles, dtype=jnp.int32)).astype(jnp.float32)
    times = jnp.einsum("pu,pv->uv", first_hot, second_hot)
    spread = (jnp.exp(closeness - 3.0) * (1.0 / math.sqrt(TILE))).astype(jnp.bfloat16)
    times = jnp.repeat(jnp.repeat(times, TILE, axis=0), TILE, axis=1).astype(jnp.bfloat16)
    weights = spread * times
    forward = jnp.dot(weights, sources, preferred_element_type=jnp.float32)
    backward = lax.dot_general(weights, cotangent, (((0,), (0,)), ((), ())), preferred_element_type=jnp.float32)
    below = shifted(backward[atom_rows:].astype(jnp.bfloat16), ("grp", "dev"), 1).astype(jnp.float32)
    near_grad = (backward[:atom_rows] + below).astype(jnp.bfloat16)
    mixed = lax.dot_general(near_grad, short_weight, (((1,), (1,)), ((), ())), preferred_element_type=jnp.float32)
    long_range = jnp.dot(table, coeffs, preferred_element_type=jnp.float32)
    message = (long_range[:, :channels] + forward).astype(jnp.bfloat16)
    embedding_grad = (long_range[:, channels:] + mixed).astype(jnp.bfloat16)
    return (message, embedding_grad)


def solution(mesh):
    split = P(("grp", "dev"), None)
    in_specs = (split, split, P(None, ("grp", "dev")), P(), split, P(("grp", "dev")), P(), P())
    return jax.shard_map(body, mesh=mesh, in_specs=in_specs, out_specs=(split, split), check_vma=False)
```

```python
import functools
import math

import jax
import jax.numpy as jnp
from jax import lax
from jax.experimental import pallas as pl
from jax.experimental.pallas import tpu as pltpu
from jax.sharding import PartitionSpec as P

TILE = 128
two_pi = 2.0 * math.pi


def shifted(value, axis, by):
    size = lax.axis_size(axis)
    return lax.ppermute(value, axis, [(i, (i + by) % size) for i in range(size)])


def cos_sin(turns):
    rest = turns - jnp.round(turns)
    angle = rest * (two_pi / 4.0)
    sq = angle * angle
    sine = angle * (1.0 + sq * (-1.0 / 6 + sq * (1.0 / 120 + sq * (-1.0 / 5040 + sq * (1.0 / 362880)))))
    cosine = 1.0 + sq * (-0.5 + sq * (1.0 / 24 + sq * (-1.0 / 720 + sq * (1.0 / 40320))))
    for _ in range(2):
        sine, cosine = 2.0 * sine * cosine, 1.0 - 2.0 * sine * sine
    return cosine, sine


def trig_table(places, wave_index):
    turns = lax.dot_general(
        places, wave_index.astype(jnp.bfloat16), (((0,), (0,)), ((), ())), preferred_element_type=jnp.float32
    )
    cosine, sine = cos_sin(turns)
    return jnp.concatenate([cosine.astype(jnp.bfloat16), sine.astype(jnp.bfloat16)], axis=1)


def reduce_kernel(groups, depth, inv_root, part_ref, sent_ref, filter_ref, left_ref, right_ref, times_ref, sources_ref, cot_ref,
                  out_ref, forward_ref, grad_ref, half_wide, half_in, half_sum, group_wide, group_in, group_sum, depth_in,
                  backward, back_out, back_in, send_sem, recv_sem):
    grp, dev = lax.axis_index("grp"), lax.axis_index("dev")
    place, core = dev // 2, dev % 2
    half = part_ref.shape[0] // 2
    rows = half // groups
    share = rows // depth
    scatter = rows % depth == 0 and share % 16 == 0
    other = {"dev": place * 2 + 1 - core}
    group_peers = [lax.rem(grp + s, groups) for s in range(1, groups)]
    place_peers = [lax.rem(place + s, depth) for s in range(1, depth)]
    group_ids = [{"grp": p} for p in group_peers]
    place_ids = [{"dev": p * 2 + core} for p in place_peers]
    used = [0]

    barrier = pltpu.get_barrier_semaphore()
    devices = lax.axis_size("dev")
    blocks = groups * devices
    after, before = (lax.rem(grp * devices + dev + step, blocks) for step in (1, blocks - 1))
    next_id, last_id = ({"grp": b // devices, "dev": lax.rem(b, devices)} for b in (after, before))
    for who in [other, *group_ids, *place_ids, next_id, last_id]:
        pl.semaphore_signal(barrier, inc=1, device_id=who, device_id_type=pl.DeviceIdType.MESH)
    pl.semaphore_wait(barrier, 3 + len(group_ids) + len(place_ids))
    atom_rows = cot_ref.shape[0]
    tiles = atom_rows // TILE
    backward[...] = jnp.zeros_like(backward)

    def near_tile(u, carry):
        here = span(u * TILE, TILE)
        closeness = jnp.dot(left_ref[here, :], right_ref[...], preferred_element_type=jnp.float32)
        spread = (jnp.exp(closeness - 3.0) * (1.0 / math.sqrt(TILE))).astype(jnp.bfloat16)
        weights = (spread.astype(jnp.float32) * times_ref[pl.ds(u, 1), :]).astype(jnp.bfloat16)
        forward_ref[here, :] = jnp.dot(weights, sources_ref[...], preferred_element_type=jnp.float32)
        backward[...] += lax.dot_general(
            weights, cot_ref[here, :], (((0,), (0,)), ((), ())), preferred_element_type=jnp.float32
        )
        return carry

    def span(start, size):
        return pl.ds(pl.multiple_of(start, 16), size)

    def exchange(moves, first=0, last=0):
        copies = []
        for source, target, who in moves:
            copies.append(pltpu.make_async_remote_copy(
                src_ref=source, dst_ref=target, send_sem=send_sem.at[used[0]], recv_sem=recv_sem.at[used[0]],
                device_id=who, device_id_type=pl.DeviceIdType.MESH,
            ))
            used[0] += 1
        for copy in copies:
            copy.start()
        if last > first:
            lax.fori_loop(first, last, near_tile, 0)
        for copy in copies:
            copy.wait()

    def filtered(total, start):
        gain = filter_ref[span(start, total.shape[0]), :]
        return (total * jnp.concatenate([gain, gain], axis=1) * inv_root).astype(jnp.bfloat16)

    exchange([(sent_ref.at[span((1 - core) * half, half)], half_in, other)], 0, tiles // 8)
    half_wide[...] = part_ref[span(core * half, half), :] + half_in[...].astype(jnp.float32)
    half_sum[...] = half_wide[...].astype(jnp.bfloat16)

    exchange([
        (half_sum.at[span(p * rows, rows)], group_in.at[s], who)
        for s, (p, who) in enumerate(zip(group_peers, group_ids))
    ], tiles // 8, tiles // 2)
    total = half_wide[span(grp * rows, rows), :]
    for s in range(groups - 1):
        total = total + group_in[s].astype(jnp.float32)
    group_wide[...] = total
    group_sum[...] = total.astype(jnp.bfloat16)

    base = core * half + grp * rows
    if scatter:
        exchange([
            (group_sum.at[span(p * share, share)], depth_in.at[s], who)
            for s, (p, who) in enumerate(zip(place_peers, place_ids))
        ], tiles // 2, tiles * 3 // 4)
        total = group_wide[span(place * share, share), :]
        for s in range(depth - 1):
            total = total + depth_in[s].astype(jnp.float32)
        mine = span(base + place * share, share)
        out_ref[mine, :] = filtered(total, grp * rows + place * share)
        exchange([(out_ref.at[mine], out_ref.at[mine], who) for who in place_ids], tiles * 3 // 4, tiles)
    else:
        exchange([(group_sum, depth_in.at[s], who) for s, who in enumerate(place_ids)], tiles // 2, tiles)
        total = group_wide[...]
        for s in range(depth - 1):
            total = total + depth_in[s].astype(jnp.float32)
        out_ref[span(base, rows), :] = filtered(total, grp * rows)
    back_out[...] = backward[atom_rows:, :].astype(jnp.bfloat16)
    back = pltpu.make_async_remote_copy(
        src_ref=back_out, dst_ref=back_in, send_sem=send_sem.at[used[0]], recv_sem=recv_sem.at[used[0]],
        device_id=next_id, device_id_type=pl.DeviceIdType.MESH,
    )
    used[0] += 1
    back.start()
    mine = span(base, rows)
    exchange([(out_ref.at[mine], out_ref.at[mine], who) for who in group_ids])
    mine = span(core * half, half)
    exchange([(out_ref.at[mine], out_ref.at[mine], other)])
    back.wait()
    grad_ref[...] = (backward[:atom_rows, :] + back_in[...].astype(jnp.float32)).astype(jnp.bfloat16)


def reduced(part, wave_filter, left, right, times, sources, cotangent, inv_root):
    groups, depth = lax.axis_size("grp"), lax.axis_size("dev") // 2
    total_rows, width = part.shape
    half = total_rows // 2
    rows = half // groups
    share = rows // depth if rows % depth == 0 and (rows // depth) % 16 == 0 else rows
    copies = 3 + 2 * (groups - 1) + 2 * (depth - 1)
    return pl.pallas_call(
        functools.partial(reduce_kernel, groups, depth, inv_root),
        out_shape=(
            jax.ShapeDtypeStruct(part.shape, jnp.bfloat16),
            jax.ShapeDtypeStruct(cotangent.shape, jnp.float32),
            jax.ShapeDtypeStruct(cotangent.shape, jnp.bfloat16),
        ),
        in_specs=[pl.BlockSpec(memory_space=pltpu.VMEM)] * 8,
        out_specs=(pl.BlockSpec(memory_space=pltpu.VMEM),) * 3,
        scratch_shapes=[
            pltpu.VMEM((half, width), jnp.float32),
            pltpu.VMEM((half, width), jnp.bfloat16),
            pltpu.VMEM((half, width), jnp.bfloat16),
            pltpu.VMEM((rows, width), jnp.float32),
            pltpu.VMEM((groups - 1, rows, width), jnp.bfloat16),
            pltpu.VMEM((rows, width), jnp.bfloat16),
            pltpu.VMEM((depth - 1, share, width), jnp.bfloat16),
            pltpu.VMEM(sources.shape, jnp.float32),
            pltpu.VMEM(cotangent.shape, jnp.bfloat16),
            pltpu.VMEM(cotangent.shape, jnp.bfloat16),
            pltpu.SemaphoreType.DMA((copies,)),
            pltpu.SemaphoreType.DMA((copies,)),
        ],
        compiler_params=pltpu.CompilerParams(collective_id=0, has_side_effects=True, vmem_limit_bytes=40 * 2**20),
        cost_estimate=pl.CostEstimate(flops=4 * part.size, bytes_accessed=8 * part.size, transcendentals=0),
    )(part, part.astype(jnp.bfloat16), wave_filter, left, right, times, sources, cotangent)


def body(embedding, cotangent, fractional, wave_index, tile_pairs, counts, wave_filter, short_weight):
    atom_rows, channels = embedding.shape
    tiles = atom_rows // TILE
    pair_rows = tile_pairs.shape[0]
    blocks = lax.axis_size("grp") * lax.axis_size("dev")
    inv_root = 1.0 / math.sqrt(atom_rows * blocks)
    above_embedding, above_places = shifted((embedding, fractional), ("grp", "dev"), -1)
    table = trig_table(fractional, wave_index)
    joined = jnp.concatenate([embedding, cotangent], axis=1)
    part = lax.dot_general(table, joined, (((0,), (0,)), ((), ())), preferred_element_type=jnp.float32)

    sources = jnp.dot(
        jnp.concatenate([embedding, above_embedding], axis=0), short_weight, preferred_element_type=jnp.float32
    ).astype(jnp.bfloat16)
    cosine, sine = cos_sin(jnp.concatenate([fractional, above_places], axis=1).astype(jnp.float32))
    waves = jnp.concatenate([cosine, sine], axis=0)
    high = lax.reduce_precision(waves, 8, 7)
    low = (waves - high).astype(jnp.bfloat16)
    high = high.astype(jnp.bfloat16)
    left = jnp.concatenate([high, high, low], axis=0)[:, :atom_rows].T
    right = jnp.concatenate([high, low, high], axis=0)
    live = (jnp.arange(pair_rows, dtype=jnp.int32) < counts[0])[:, None]
    first_hot = ((tile_pairs[:, :1] == jnp.arange(tiles, dtype=jnp.int32)) & live).astype(jnp.float32)
    second_hot = (tile_pairs[:, 1:] == jnp.arange(2 * tiles, dtype=jnp.int32)).astype(jnp.float32)
    times = jnp.einsum("pu,pv->uv", first_hot, second_hot)
    times = jnp.repeat(times, TILE, axis=1)
    coeffs, forward, near_grad = reduced(part, wave_filter, left, right, times, sources, cotangent, inv_root)
    mixed = lax.dot_general(near_grad, short_weight, (((1,), (1,)), ((), ())), preferred_element_type=jnp.float32)
    long_range = jnp.dot(table, coeffs, preferred_element_type=jnp.float32)
    message = (long_range[:, :channels] + forward).astype(jnp.bfloat16)
    embedding_grad = (long_range[:, channels:] + mixed).astype(jnp.bfloat16)
    return (message, embedding_grad)


def solution(mesh):
    split = P(("grp", "dev"), None)
    in_specs = (split, split, P(None, ("grp", "dev")), P(), split, P(("grp", "dev")), P(), P())
    return jax.shard_map(body, mesh=mesh, in_specs=in_specs, out_specs=(split, split), check_vma=False)
```

```python
import functools
import math

import jax
import jax.numpy as jnp
from jax import lax
from jax.experimental import pallas as pl
from jax.experimental.pallas import tpu as pltpu
from jax.sharding import PartitionSpec as P

TILE = 128
two_pi = 2.0 * math.pi


def cos_sin(turns):
    rest = turns - jnp.round(turns)
    angle = rest * (two_pi / 4.0)
    sq = angle * angle
    sine = angle * (1.0 + sq * (-1.0 / 6 + sq * (1.0 / 120 + sq * (-1.0 / 5040 + sq * (1.0 / 362880)))))
    cosine = 1.0 + sq * (-0.5 + sq * (1.0 / 24 + sq * (-1.0 / 720 + sq * (1.0 / 40320))))
    for _ in range(2):
        sine, cosine = 2.0 * sine * cosine, 1.0 - 2.0 * sine * sine
    return cosine, sine


def trig_table(places, wave_index):
    turns = lax.dot_general(
        places, wave_index.astype(jnp.bfloat16), (((0,), (0,)), ((), ())), preferred_element_type=jnp.float32
    )
    cosine, sine = cos_sin(turns)
    return jnp.concatenate([cosine.astype(jnp.bfloat16), sine.astype(jnp.bfloat16)], axis=1)


def reduce_kernel(groups, depth, inv_root, part_ref, sent_ref, filter_ref, left_ref, right_ref, times_ref, sources_ref, cot_ref,
                  out_ref, forward_ref, grad_ref, half_wide, half_in, half_sum, group_wide, group_in, group_sum, depth_in,
                  backward, back_out, back_in, all_sources, all_right, send_sem, recv_sem):
    grp, dev = lax.axis_index("grp"), lax.axis_index("dev")
    place, core = dev // 2, dev % 2
    half = part_ref.shape[0] // 2
    rows = half // groups
    share = rows // depth
    scatter = rows % depth == 0 and share % 16 == 0
    other = {"dev": place * 2 + 1 - core}
    group_peers = [lax.rem(grp + s, groups) for s in range(1, groups)]
    place_peers = [lax.rem(place + s, depth) for s in range(1, depth)]
    group_ids = [{"grp": p} for p in group_peers]
    place_ids = [{"dev": p * 2 + core} for p in place_peers]
    used = [0]

    barrier = pltpu.get_barrier_semaphore()
    devices = lax.axis_size("dev")
    blocks = groups * devices
    after, before = (lax.rem(grp * devices + dev + step, blocks) for step in (1, blocks - 1))
    next_id, last_id = ({"grp": b // devices, "dev": lax.rem(b, devices)} for b in (after, before))
    for who in [other, *group_ids, *place_ids, next_id, last_id]:
        pl.semaphore_signal(barrier, inc=1, device_id=who, device_id_type=pl.DeviceIdType.MESH)
    pl.semaphore_wait(barrier, 3 + len(group_ids) + len(place_ids))
    atom_rows = cot_ref.shape[0]
    tiles = atom_rows // TILE
    backward[...] = jnp.zeros_like(backward)
    all_sources[:atom_rows, :] = sources_ref[...]
    all_right[:, :atom_rows] = right_ref[...]

    def near_tile(u, carry):
        here = span(u * TILE, TILE)
        closeness = jnp.dot(left_ref[here, :], all_right[...], preferred_element_type=jnp.float32)
        spread = (jnp.exp(closeness - 3.0) * (1.0 / math.sqrt(TILE))).astype(jnp.bfloat16)
        weights = (spread.astype(jnp.float32) * times_ref[pl.ds(u, 1), :]).astype(jnp.bfloat16)
        forward_ref[here, :] = jnp.dot(weights, all_sources[...], preferred_element_type=jnp.float32)
        backward[...] += lax.dot_general(
            weights, cot_ref[here, :], (((0,), (0,)), ((), ())), preferred_element_type=jnp.float32
        )
        return carry

    def span(start, size):
        return pl.ds(pl.multiple_of(start, 16), size)

    def exchange(moves, first=0, last=0):
        copies = []
        for source, target, who in moves:
            copies.append(pltpu.make_async_remote_copy(
                src_ref=source, dst_ref=target, send_sem=send_sem.at[used[0]], recv_sem=recv_sem.at[used[0]],
                device_id=who, device_id_type=pl.DeviceIdType.MESH,
            ))
            used[0] += 1
        for copy in copies:
            copy.start()
        if last > first:
            lax.fori_loop(first, last, near_tile, 0)
        for copy in copies:
            copy.wait()

    def filtered(total, start):
        gain = filter_ref[span(start, total.shape[0]), :]
        return (total * jnp.concatenate([gain, gain], axis=1) * inv_root).astype(jnp.bfloat16)

    exchange([(sent_ref.at[span((1 - core) * half, half)], half_in, other),
        (sources_ref, all_sources.at[atom_rows:, :], last_id),
        (right_ref, all_right.at[:, atom_rows:], last_id),
    ])
    half_wide[...] = part_ref[span(core * half, half), :] + half_in[...].astype(jnp.float32)
    half_sum[...] = half_wide[...].astype(jnp.bfloat16)

    exchange([
        (half_sum.at[span(p * rows, rows)], group_in.at[s], who)
        for s, (p, who) in enumerate(zip(group_peers, group_ids))
    ], 0, tiles // 2)
    total = half_wide[span(grp * rows, rows), :]
    for s in range(groups - 1):
        total = total + group_in[s].astype(jnp.float32)
    group_wide[...] = total
    group_sum[...] = total.astype(jnp.bfloat16)

    base = core * half + grp * rows
    if scatter:
        exchange([
            (group_sum.at[span(p * share, share)], depth_in.at[s], who)
            for s, (p, who) in enumerate(zip(place_peers, place_ids))
        ], tiles // 2, tiles * 3 // 4)
        total = group_wide[span(place * share, share), :]
        for s in range(depth - 1):
            total = total + depth_in[s].astype(jnp.float32)
        mine = span(base + place * share, share)
        out_ref[mine, :] = filtered(total, grp * rows + place * share)
        exchange([(out_ref.at[mine], out_ref.at[mine], who) for who in place_ids], tiles * 3 // 4, tiles)
    else:
        exchange([(group_sum, depth_in.at[s], who) for s, who in enumerate(place_ids)], tiles // 2, tiles)
        total = group_wide[...]
        for s in range(depth - 1):
            total = total + depth_in[s].astype(jnp.float32)
        out_ref[span(base, rows), :] = filtered(total, grp * rows)
    back_out[...] = backward[atom_rows:, :].astype(jnp.bfloat16)
    back = pltpu.make_async_remote_copy(
        src_ref=back_out, dst_ref=back_in, send_sem=send_sem.at[used[0]], recv_sem=recv_sem.at[used[0]],
        device_id=next_id, device_id_type=pl.DeviceIdType.MESH,
    )
    used[0] += 1
    back.start()
    mine = span(base, rows)
    exchange([(out_ref.at[mine], out_ref.at[mine], who) for who in group_ids])
    mine = span(core * half, half)
    exchange([(out_ref.at[mine], out_ref.at[mine], other)])
    back.wait()
    grad_ref[...] = (backward[:atom_rows, :] + back_in[...].astype(jnp.float32)).astype(jnp.bfloat16)


def reduced(part, wave_filter, left, right, times, sources, cotangent, inv_root):
    groups, depth = lax.axis_size("grp"), lax.axis_size("dev") // 2
    total_rows, width = part.shape
    half = total_rows // 2
    rows = half // groups
    share = rows // depth if rows % depth == 0 and (rows // depth) % 16 == 0 else rows
    copies = 5 + 2 * (groups - 1) + 2 * (depth - 1)
    return pl.pallas_call(
        functools.partial(reduce_kernel, groups, depth, inv_root),
        out_shape=(
            jax.ShapeDtypeStruct(part.shape, jnp.bfloat16),
            jax.ShapeDtypeStruct(cotangent.shape, jnp.float32),
            jax.ShapeDtypeStruct(cotangent.shape, jnp.bfloat16),
        ),
        in_specs=[pl.BlockSpec(memory_space=pltpu.VMEM)] * 8,
        out_specs=(pl.BlockSpec(memory_space=pltpu.VMEM),) * 3,
        scratch_shapes=[
            pltpu.VMEM((half, width), jnp.float32),
            pltpu.VMEM((half, width), jnp.bfloat16),
            pltpu.VMEM((half, width), jnp.bfloat16),
            pltpu.VMEM((rows, width), jnp.float32),
            pltpu.VMEM((groups - 1, rows, width), jnp.bfloat16),
            pltpu.VMEM((rows, width), jnp.bfloat16),
            pltpu.VMEM((depth - 1, share, width), jnp.bfloat16),
            pltpu.VMEM((2 * sources.shape[0], sources.shape[1]), jnp.float32),
            pltpu.VMEM(cotangent.shape, jnp.bfloat16),
            pltpu.VMEM(cotangent.shape, jnp.bfloat16),
            pltpu.VMEM((2 * sources.shape[0], sources.shape[1]), jnp.bfloat16),
            pltpu.VMEM((right.shape[0], 2 * right.shape[1]), jnp.bfloat16),
            pltpu.SemaphoreType.DMA((copies,)),
            pltpu.SemaphoreType.DMA((copies,)),
        ],
        compiler_params=pltpu.CompilerParams(collective_id=0, has_side_effects=True, vmem_limit_bytes=40 * 2**20),
        cost_estimate=pl.CostEstimate(flops=4 * part.size, bytes_accessed=8 * part.size, transcendentals=0),
    )(part, part.astype(jnp.bfloat16), wave_filter, left, right, times, sources, cotangent)


def body(embedding, cotangent, fractional, wave_index, tile_pairs, counts, wave_filter, short_weight):
    atom_rows, channels = embedding.shape
    tiles = atom_rows // TILE
    pair_rows = tile_pairs.shape[0]
    blocks = lax.axis_size("grp") * lax.axis_size("dev")
    inv_root = 1.0 / math.sqrt(atom_rows * blocks)
    table = trig_table(fractional, wave_index)
    joined = jnp.concatenate([embedding, cotangent], axis=1)
    part = lax.dot_general(table, joined, (((0,), (0,)), ((), ())), preferred_element_type=jnp.float32)

    sources = jnp.dot(
        embedding, short_weight, preferred_element_type=jnp.float32
    ).astype(jnp.bfloat16)
    cosine, sine = cos_sin(fractional.astype(jnp.float32))
    waves = jnp.concatenate([cosine, sine], axis=0)
    high = lax.reduce_precision(waves, 8, 7)
    low = (waves - high).astype(jnp.bfloat16)
    high = high.astype(jnp.bfloat16)
    fill = jnp.zeros((-3 * high.shape[0] % 16, atom_rows), jnp.bfloat16)
    left = jnp.concatenate([high, high, low, fill], axis=0).T
    right = jnp.concatenate([high, low, high, fill], axis=0)
    live = (jnp.arange(pair_rows, dtype=jnp.int32) < counts[0])[:, None]
    first_hot = ((tile_pairs[:, :1] == jnp.arange(tiles, dtype=jnp.int32)) & live).astype(jnp.float32)
    second_hot = (tile_pairs[:, 1:] == jnp.arange(2 * tiles, dtype=jnp.int32)).astype(jnp.float32)
    times = jnp.einsum("pu,pv->uv", first_hot, second_hot)
    times = jnp.repeat(times, TILE, axis=1)
    coeffs, forward, near_grad = reduced(part, wave_filter, left, right, times, sources, cotangent, inv_root)
    mixed = lax.dot_general(near_grad, short_weight, (((1,), (1,)), ((), ())), preferred_element_type=jnp.float32)
    long_range = jnp.dot(table, coeffs, preferred_element_type=jnp.float32)
    message = (long_range[:, :channels] + forward).astype(jnp.bfloat16)
    embedding_grad = (long_range[:, channels:] + mixed).astype(jnp.bfloat16)
    return (message, embedding_grad)


def solution(mesh):
    split = P(("grp", "dev"), None)
    in_specs = (split, split, P(None, ("grp", "dev")), P(), split, P(("grp", "dev")), P(), P())
    return jax.shard_map(body, mesh=mesh, in_specs=in_specs, out_specs=(split, split), check_vma=False)
```

```python
import functools
import math

import jax
import jax.numpy as jnp
from jax import lax
from jax.experimental import pallas as pl
from jax.experimental.pallas import tpu as pltpu
from jax.sharding import PartitionSpec as P

TILE = 128
two_pi = 2.0 * math.pi


def cos_sin(turns):
    rest = turns - jnp.round(turns)
    angle = rest * (two_pi / 4.0)
    sq = angle * angle
    sine = angle * (1.0 + sq * (-1.0 / 6 + sq * (1.0 / 120 + sq * (-1.0 / 5040 + sq * (1.0 / 362880)))))
    cosine = 1.0 + sq * (-0.5 + sq * (1.0 / 24 + sq * (-1.0 / 720 + sq * (1.0 / 40320))))
    for _ in range(2):
        sine, cosine = 2.0 * sine * cosine, 1.0 - 2.0 * sine * sine
    return cosine, sine


def trig_table(places, wave_index):
    turns = lax.dot_general(
        places, wave_index.astype(jnp.bfloat16), (((0,), (0,)), ((), ())), preferred_element_type=jnp.float32
    )
    cosine, sine = cos_sin(turns)
    return jnp.concatenate([cosine.astype(jnp.bfloat16), sine.astype(jnp.bfloat16)], axis=1)


def reduce_kernel(groups, depth, inv_root, part_ref, sent_ref, filter_ref, left_ref, right_ref, times_ref, sources_ref, cot_ref,
                  out_ref, forward_ref, grad_ref, half_wide, half_in, half_sum, group_wide, group_in, group_sum, depth_in,
                  backward, back_out, back_in, sources_in, right_in, send_sem, recv_sem):
    grp, dev = lax.axis_index("grp"), lax.axis_index("dev")
    place, core = dev // 2, dev % 2
    half = part_ref.shape[0] // 2
    rows = half // groups
    share = rows // depth
    scatter = rows % depth == 0 and share % 16 == 0
    other = {"dev": place * 2 + 1 - core}
    group_peers = [lax.rem(grp + s, groups) for s in range(1, groups)]
    place_peers = [lax.rem(place + s, depth) for s in range(1, depth)]
    group_ids = [{"grp": p} for p in group_peers]
    place_ids = [{"dev": p * 2 + core} for p in place_peers]
    used = [0]

    barrier = pltpu.get_barrier_semaphore()
    devices = lax.axis_size("dev")
    blocks = groups * devices
    after, before = (lax.rem(grp * devices + dev + step, blocks) for step in (1, blocks - 1))
    next_id, last_id = ({"grp": b // devices, "dev": lax.rem(b, devices)} for b in (after, before))
    for who in [other, *group_ids, *place_ids, next_id, last_id]:
        pl.semaphore_signal(barrier, inc=1, device_id=who, device_id_type=pl.DeviceIdType.MESH)
    pl.semaphore_wait(barrier, 3 + len(group_ids) + len(place_ids))
    atom_rows = cot_ref.shape[0]
    tiles = atom_rows // TILE
    backward[...] = jnp.zeros_like(backward)
    forward_ref[...] = jnp.zeros_like(forward_ref)

    def near_tiles(side, first, last):
        waves, values = ((right_ref, sources_ref), (right_in, sources_in))[side]
        there = pl.ds(side * atom_rows, atom_rows)

        def near_tile(u, carry):
            here = span(u * TILE, TILE)
            closeness = jnp.dot(left_ref[here, :], waves[...], preferred_element_type=jnp.float32)
            spread = (jnp.exp(closeness - 3.0) * (1.0 / math.sqrt(TILE))).astype(jnp.bfloat16)
            weights = (spread.astype(jnp.float32) * times_ref[pl.ds(u, 1), there]).astype(jnp.bfloat16)
            forward_ref[here, :] += jnp.dot(weights, values[...], preferred_element_type=jnp.float32)
            backward[there, :] += lax.dot_general(
                weights, cot_ref[here, :], (((0,), (0,)), ((), ())), preferred_element_type=jnp.float32
            )
            return carry

        lax.fori_loop(first, last, near_tile, 0)

    def span(start, size):
        return pl.ds(pl.multiple_of(start, 16), size)

    def exchange(moves, side=0, first=0, last=0, wait=True):
        copies = []
        for source, target, who in moves:
            copies.append(pltpu.make_async_remote_copy(
                src_ref=source, dst_ref=target, send_sem=send_sem.at[used[0]], recv_sem=recv_sem.at[used[0]],
                device_id=who, device_id_type=pl.DeviceIdType.MESH,
            ))
            used[0] += 1
        for copy in copies:
            copy.start()
        if last > first:
            near_tiles(side, first, last)
        if wait:
            for copy in copies:
                copy.wait()
        return copies

    def filtered(total, start):
        gain = filter_ref[span(start, total.shape[0]), :]
        return (total * jnp.concatenate([gain, gain], axis=1) * inv_root).astype(jnp.bfloat16)

    neighbour = exchange([(sources_ref, sources_in, last_id), (right_ref, right_in, last_id)], wait=False)
    exchange([(sent_ref.at[span((1 - core) * half, half)], half_in, other)], 0, 0, tiles // 4)
    half_wide[...] = part_ref[span(core * half, half), :] + half_in[...].astype(jnp.float32)
    half_sum[...] = half_wide[...].astype(jnp.bfloat16)

    exchange([
        (half_sum.at[span(p * rows, rows)], group_in.at[s], who)
        for s, (p, who) in enumerate(zip(group_peers, group_ids))
    ], 0, tiles // 4, tiles * 7 // 8)
    for copy in neighbour:
        copy.wait()
    total = half_wide[span(grp * rows, rows), :]
    for s in range(groups - 1):
        total = total + group_in[s].astype(jnp.float32)
    group_wide[...] = total
    group_sum[...] = total.astype(jnp.bfloat16)

    base = core * half + grp * rows
    if scatter:
        exchange([
            (group_sum.at[span(p * share, share)], depth_in.at[s], who)
            for s, (p, who) in enumerate(zip(place_peers, place_ids))
        ], 1, 0, tiles // 2)
        total = group_wide[span(place * share, share), :]
        for s in range(depth - 1):
            total = total + depth_in[s].astype(jnp.float32)
        mine = span(base + place * share, share)
        out_ref[mine, :] = filtered(total, grp * rows + place * share)
        exchange([(out_ref.at[mine], out_ref.at[mine], who) for who in place_ids], 1, tiles // 2, tiles)
    else:
        exchange([(group_sum, depth_in.at[s], who) for s, who in enumerate(place_ids)], 1, 0, tiles)
        total = group_wide[...]
        for s in range(depth - 1):
            total = total + depth_in[s].astype(jnp.float32)
        out_ref[span(base, rows), :] = filtered(total, grp * rows)
    back_out[...] = backward[atom_rows:, :].astype(jnp.bfloat16)
    back = pltpu.make_async_remote_copy(
        src_ref=back_out, dst_ref=back_in, send_sem=send_sem.at[used[0]], recv_sem=recv_sem.at[used[0]],
        device_id=next_id, device_id_type=pl.DeviceIdType.MESH,
    )
    used[0] += 1
    back.start()
    mine = span(base, rows)
    exchange([(out_ref.at[mine], out_ref.at[mine], who) for who in group_ids], 0, tiles * 7 // 8, tiles)
    mine = span(core * half, half)
    exchange([(out_ref.at[mine], out_ref.at[mine], other)])
    back.wait()
    grad_ref[...] = (backward[:atom_rows, :] + back_in[...].astype(jnp.float32)).astype(jnp.bfloat16)


def reduced(part, wave_filter, left, right, times, sources, cotangent, inv_root):
    groups, depth = lax.axis_size("grp"), lax.axis_size("dev") // 2
    total_rows, width = part.shape
    half = total_rows // 2
    rows = half // groups
    share = rows // depth if rows % depth == 0 and (rows // depth) % 16 == 0 else rows
    copies = 5 + 2 * (groups - 1) + 2 * (depth - 1)
    return pl.pallas_call(
        functools.partial(reduce_kernel, groups, depth, inv_root),
        out_shape=(
            jax.ShapeDtypeStruct(part.shape, jnp.bfloat16),
            jax.ShapeDtypeStruct(cotangent.shape, jnp.float32),
            jax.ShapeDtypeStruct(cotangent.shape, jnp.bfloat16),
        ),
        in_specs=[pl.BlockSpec(memory_space=pltpu.VMEM)] * 8,
        out_specs=(pl.BlockSpec(memory_space=pltpu.VMEM),) * 3,
        scratch_shapes=[
            pltpu.VMEM((half, width), jnp.float32),
            pltpu.VMEM((half, width), jnp.bfloat16),
            pltpu.VMEM((half, width), jnp.bfloat16),
            pltpu.VMEM((rows, width), jnp.float32),
            pltpu.VMEM((groups - 1, rows, width), jnp.bfloat16),
            pltpu.VMEM((rows, width), jnp.bfloat16),
            pltpu.VMEM((depth - 1, share, width), jnp.bfloat16),
            pltpu.VMEM((2 * sources.shape[0], sources.shape[1]), jnp.float32),
            pltpu.VMEM(cotangent.shape, jnp.bfloat16),
            pltpu.VMEM(cotangent.shape, jnp.bfloat16),
            pltpu.VMEM(sources.shape, jnp.bfloat16),
            pltpu.VMEM(right.shape, jnp.bfloat16),
            pltpu.SemaphoreType.DMA((copies,)),
            pltpu.SemaphoreType.DMA((copies,)),
        ],
        compiler_params=pltpu.CompilerParams(collective_id=0, has_side_effects=True, vmem_limit_bytes=40 * 2**20),
        cost_estimate=pl.CostEstimate(flops=4 * part.size, bytes_accessed=8 * part.size, transcendentals=0),
    )(part, part.astype(jnp.bfloat16), wave_filter, left, right, times, sources, cotangent)


def body(embedding, cotangent, fractional, wave_index, tile_pairs, counts, wave_filter, short_weight):
    atom_rows, channels = embedding.shape
    tiles = atom_rows // TILE
    pair_rows = tile_pairs.shape[0]
    blocks = lax.axis_size("grp") * lax.axis_size("dev")
    inv_root = 1.0 / math.sqrt(atom_rows * blocks)
    table = trig_table(fractional, wave_index)
    joined = jnp.concatenate([embedding, cotangent], axis=1)
    part = lax.dot_general(table, joined, (((0,), (0,)), ((), ())), preferred_element_type=jnp.float32)

    sources = jnp.dot(
        embedding, short_weight, preferred_element_type=jnp.float32
    ).astype(jnp.bfloat16)
    cosine, sine = cos_sin(fractional.astype(jnp.float32))
    waves = jnp.concatenate([cosine, sine], axis=0)
    high = lax.reduce_precision(waves, 8, 7)
    low = (waves - high).astype(jnp.bfloat16)
    high = high.astype(jnp.bfloat16)
    fill = jnp.zeros((-3 * high.shape[0] % 16, atom_rows), jnp.bfloat16)
    left = jnp.concatenate([high, high, low, fill], axis=0).T
    right = jnp.concatenate([high, low, high, fill], axis=0)
    live = (jnp.arange(pair_rows, dtype=jnp.int32) < counts[0])[:, None]
    first_hot = ((tile_pairs[:, :1] == jnp.arange(tiles, dtype=jnp.int32)) & live).astype(jnp.float32)
    second_hot = (tile_pairs[:, 1:] == jnp.arange(2 * tiles, dtype=jnp.int32)).astype(jnp.float32)
    times = jnp.einsum("pu,pv->uv", first_hot, second_hot)
    times = jnp.repeat(times, TILE, axis=1)
    coeffs, forward, near_grad = reduced(part, wave_filter, left, right, times, sources, cotangent, inv_root)
    mixed = lax.dot_general(near_grad, short_weight, (((1,), (1,)), ((), ())), preferred_element_type=jnp.float32)
    long_range = jnp.dot(table, coeffs, preferred_element_type=jnp.float32)
    message = (long_range[:, :channels] + forward).astype(jnp.bfloat16)
    embedding_grad = (long_range[:, channels:] + mixed).astype(jnp.bfloat16)
    return (message, embedding_grad)


def solution(mesh):
    split = P(("grp", "dev"), None)
    in_specs = (split, split, P(None, ("grp", "dev")), P(), split, P(("grp", "dev")), P(), P())
    return jax.shard_map(body, mesh=mesh, in_specs=in_specs, out_specs=(split, split), check_vma=False)
```

```python
import functools
import math

import jax
import jax.numpy as jnp
from jax import lax
from jax.experimental import pallas as pl
from jax.experimental.pallas import tpu as pltpu
from jax.sharding import PartitionSpec as P

TILE = 128
two_pi = 2.0 * math.pi


def cos_sin(turns):
    rest = turns - jnp.round(turns)
    angle = rest * (two_pi / 4.0)
    sq = angle * angle
    sine = angle * (1.0 + sq * (-1.0 / 6 + sq * (1.0 / 120 + sq * (-1.0 / 5040 + sq * (1.0 / 362880)))))
    cosine = 1.0 + sq * (-0.5 + sq * (1.0 / 24 + sq * (-1.0 / 720 + sq * (1.0 / 40320))))
    for _ in range(2):
        sine, cosine = 2.0 * sine * cosine, 1.0 - 2.0 * sine * sine
    return cosine, sine


def trig_table(places, wave_index):
    turns = lax.dot_general(
        places, wave_index.astype(jnp.bfloat16), (((0,), (0,)), ((), ())), preferred_element_type=jnp.float32
    )
    cosine, sine = cos_sin(turns)
    return jnp.concatenate([cosine.astype(jnp.bfloat16), sine.astype(jnp.bfloat16)], axis=1)


def reduce_kernel(groups, depth, inv_root, part_ref, sent_ref, filter_ref, left_ref, right_ref, times_ref, sources_ref, cot_ref,
                  out_ref, forward_ref, grad_ref, half_wide, half_in, half_sum, group_wide, group_in, group_sum, depth_in,
                  backward, back_out, back_in, sources_in, right_in, send_sem, recv_sem):
    grp, dev = lax.axis_index("grp"), lax.axis_index("dev")
    place, core = dev // 2, dev % 2
    half = part_ref.shape[0] // 2
    rows = half // groups
    share = rows // depth
    scatter = rows % depth == 0 and share % 16 == 0
    other = {"dev": place * 2 + 1 - core}
    group_peers = [lax.rem(grp + s, groups) for s in range(1, groups)]
    place_peers = [lax.rem(place + s, depth) for s in range(1, depth)]
    group_ids = [{"grp": p} for p in group_peers]
    place_ids = [{"dev": p * 2 + core} for p in place_peers]
    used = [0]

    barrier = pltpu.get_barrier_semaphore()
    devices = lax.axis_size("dev")
    blocks = groups * devices
    after, before = (lax.rem(grp * devices + dev + step, blocks) for step in (1, blocks - 1))
    next_id, last_id = ({"grp": b // devices, "dev": lax.rem(b, devices)} for b in (after, before))
    for who in [other, *group_ids, *place_ids, next_id, last_id]:
        pl.semaphore_signal(barrier, inc=1, device_id=who, device_id_type=pl.DeviceIdType.MESH)
    pl.semaphore_wait(barrier, 3 + len(group_ids) + len(place_ids))
    atom_rows = cot_ref.shape[0]
    tiles = atom_rows // TILE
    backward[...] = jnp.zeros_like(backward)
    forward_ref[...] = jnp.zeros_like(forward_ref)

    def near_tiles(side, first, last):
        waves, values = ((right_ref, sources_ref), (right_in, sources_in))[side]
        there = pl.ds(side * atom_rows, atom_rows)

        def near_tile(u, carry):
            here = span(u * TILE, TILE)
            closeness = jnp.dot(left_ref[here, :], waves[...], preferred_element_type=jnp.float32)
            spread = (jnp.exp(closeness - 3.0) * (1.0 / math.sqrt(TILE))).astype(jnp.bfloat16)
            weights = (spread.astype(jnp.float32) * times_ref[pl.ds(u, 1), there]).astype(jnp.bfloat16)
            forward_ref[here, :] += jnp.dot(weights, values[...], preferred_element_type=jnp.float32)
            backward[there, :] += lax.dot_general(
                weights, cot_ref[here, :], (((0,), (0,)), ((), ())), preferred_element_type=jnp.float32
            )
            return carry

        lax.fori_loop(first, last, near_tile, 0)

    def span(start, size):
        return pl.ds(pl.multiple_of(start, 16), size)

    def exchange(moves, side=0, first=0, last=0, wait=True):
        copies = []
        for source, target, who in moves:
            copies.append(pltpu.make_async_remote_copy(
                src_ref=source, dst_ref=target, send_sem=send_sem.at[used[0]], recv_sem=recv_sem.at[used[0]],
                device_id=who, device_id_type=pl.DeviceIdType.MESH,
            ))
            used[0] += 1
        for copy in copies:
            copy.start()
        if last > first:
            near_tiles(side, first, last)
        if wait:
            for copy in copies:
                copy.wait()
        return copies

    def filtered(total, start):
        gain = filter_ref[span(start, total.shape[0]), :]
        return (total * jnp.concatenate([gain, gain], axis=1) * inv_root).astype(jnp.bfloat16)

    neighbour = exchange([(sources_ref, sources_in, last_id), (right_ref, right_in, last_id)], wait=False)
    exchange([(sent_ref.at[span((1 - core) * half, half)], half_in, other)], 0, 0, tiles // 4)
    half_wide[...] = part_ref[span(core * half, half), :] + half_in[...].astype(jnp.float32)
    half_sum[...] = half_wide[...].astype(jnp.bfloat16)

    pieces = exchange([
        (half_sum.at[span(p * rows, rows)], group_in.at[s], who)
        for s, (p, who) in enumerate(zip(group_peers, group_ids))
    ], 0, tiles // 4, tiles * 5 // 8, wait=False)
    for copy in neighbour:
        copy.wait()
    near_tiles(1, 0, tiles // 4)
    for copy in pieces:
        copy.wait()
    total = half_wide[span(grp * rows, rows), :]
    for s in range(groups - 1):
        total = total + group_in[s].astype(jnp.float32)
    group_wide[...] = total
    group_sum[...] = total.astype(jnp.bfloat16)

    base = core * half + grp * rows
    if scatter:
        exchange([
            (group_sum.at[span(p * share, share)], depth_in.at[s], who)
            for s, (p, who) in enumerate(zip(place_peers, place_ids))
        ], 1, tiles // 4, tiles * 5 // 8)
        total = group_wide[span(place * share, share), :]
        for s in range(depth - 1):
            total = total + depth_in[s].astype(jnp.float32)
        mine = span(base + place * share, share)
        out_ref[mine, :] = filtered(total, grp * rows + place * share)
        exchange([(out_ref.at[mine], out_ref.at[mine], who) for who in place_ids], 1, tiles * 5 // 8, tiles)
    else:
        exchange([(group_sum, depth_in.at[s], who) for s, who in enumerate(place_ids)], 1, tiles // 4, tiles)
        total = group_wide[...]
        for s in range(depth - 1):
            total = total + depth_in[s].astype(jnp.float32)
        out_ref[span(base, rows), :] = filtered(total, grp * rows)
    back_out[...] = backward[atom_rows:, :].astype(jnp.bfloat16)
    back = pltpu.make_async_remote_copy(
        src_ref=back_out, dst_ref=back_in, send_sem=send_sem.at[used[0]], recv_sem=recv_sem.at[used[0]],
        device_id=next_id, device_id_type=pl.DeviceIdType.MESH,
    )
    used[0] += 1
    back.start()
    mine = span(base, rows)
    pieces = exchange([(out_ref.at[mine], out_ref.at[mine], who) for who in group_ids], wait=False)
    passed = exchange([(out_ref.at[mine], out_ref.at[mine], other)], 0, tiles * 5 // 8, tiles, wait=False)
    for s, copy in enumerate(pieces):
        copy.wait()
        here = span(core * half + lax.rem(grp + groups - 1 - s, groups) * rows, rows)
        passed += exchange([(out_ref.at[here], out_ref.at[here], other)], wait=False)
    for copy in passed:
        copy.wait()
    back.wait()
    grad_ref[...] = (backward[:atom_rows, :] + back_in[...].astype(jnp.float32)).astype(jnp.bfloat16)


def reduced(part, wave_filter, left, right, times, sources, cotangent, inv_root):
    groups, depth = lax.axis_size("grp"), lax.axis_size("dev") // 2
    total_rows, width = part.shape
    half = total_rows // 2
    rows = half // groups
    share = rows // depth if rows % depth == 0 and (rows // depth) % 16 == 0 else rows
    copies = 5 + 3 * (groups - 1) + 2 * (depth - 1)
    return pl.pallas_call(
        functools.partial(reduce_kernel, groups, depth, inv_root),
        out_shape=(
            jax.ShapeDtypeStruct(part.shape, jnp.bfloat16),
            jax.ShapeDtypeStruct(cotangent.shape, jnp.float32),
            jax.ShapeDtypeStruct(cotangent.shape, jnp.bfloat16),
        ),
        in_specs=[pl.BlockSpec(memory_space=pltpu.VMEM)] * 8,
        out_specs=(pl.BlockSpec(memory_space=pltpu.VMEM),) * 3,
        scratch_shapes=[
            pltpu.VMEM((half, width), jnp.float32),
            pltpu.VMEM((half, width), jnp.bfloat16),
            pltpu.VMEM((half, width), jnp.bfloat16),
            pltpu.VMEM((rows, width), jnp.float32),
            pltpu.VMEM((groups - 1, rows, width), jnp.bfloat16),
            pltpu.VMEM((rows, width), jnp.bfloat16),
            pltpu.VMEM((depth - 1, share, width), jnp.bfloat16),
            pltpu.VMEM((2 * sources.shape[0], sources.shape[1]), jnp.float32),
            pltpu.VMEM(cotangent.shape, jnp.bfloat16),
            pltpu.VMEM(cotangent.shape, jnp.bfloat16),
            pltpu.VMEM(sources.shape, jnp.bfloat16),
            pltpu.VMEM(right.shape, jnp.bfloat16),
            pltpu.SemaphoreType.DMA((copies,)),
            pltpu.SemaphoreType.DMA((copies,)),
        ],
        compiler_params=pltpu.CompilerParams(collective_id=0, has_side_effects=True, vmem_limit_bytes=40 * 2**20),
        cost_estimate=pl.CostEstimate(flops=4 * part.size, bytes_accessed=8 * part.size, transcendentals=0),
    )(part, part.astype(jnp.bfloat16), wave_filter, left, right, times, sources, cotangent)


def body(embedding, cotangent, fractional, wave_index, tile_pairs, counts, wave_filter, short_weight):
    atom_rows, channels = embedding.shape
    tiles = atom_rows // TILE
    pair_rows = tile_pairs.shape[0]
    blocks = lax.axis_size("grp") * lax.axis_size("dev")
    inv_root = 1.0 / math.sqrt(atom_rows * blocks)
    table = trig_table(fractional, wave_index)
    joined = jnp.concatenate([embedding, cotangent], axis=1)
    part = lax.dot_general(table, joined, (((0,), (0,)), ((), ())), preferred_element_type=jnp.float32)

    sources = jnp.dot(
        embedding, short_weight, preferred_element_type=jnp.float32
    ).astype(jnp.bfloat16)
    cosine, sine = cos_sin(fractional.astype(jnp.float32))
    waves = jnp.concatenate([cosine, sine], axis=0)
    high = lax.reduce_precision(waves, 8, 7)
    low = (waves - high).astype(jnp.bfloat16)
    high = high.astype(jnp.bfloat16)
    fill = jnp.zeros((-3 * high.shape[0] % 16, atom_rows), jnp.bfloat16)
    left = jnp.concatenate([high, high, low, fill], axis=0).T
    right = jnp.concatenate([high, low, high, fill], axis=0)
    live = (jnp.arange(pair_rows, dtype=jnp.int32) < counts[0])[:, None]
    first_hot = ((tile_pairs[:, :1] == jnp.arange(tiles, dtype=jnp.int32)) & live).astype(jnp.float32)
    second_hot = (tile_pairs[:, 1:] == jnp.arange(2 * tiles, dtype=jnp.int32)).astype(jnp.float32)
    times = jnp.einsum("pu,pv->uv", first_hot, second_hot)
    times = jnp.repeat(times, TILE, axis=1)
    coeffs, forward, near_grad = reduced(part, wave_filter, left, right, times, sources, cotangent, inv_root)
    mixed = lax.dot_general(near_grad, short_weight, (((1,), (1,)), ((), ())), preferred_element_type=jnp.float32)
    long_range = jnp.dot(table, coeffs, preferred_element_type=jnp.float32)
    message = (long_range[:, :channels] + forward).astype(jnp.bfloat16)
    embedding_grad = (long_range[:, channels:] + mixed).astype(jnp.bfloat16)
    return (message, embedding_grad)


def solution(mesh):
    split = P(("grp", "dev"), None)
    in_specs = (split, split, P(None, ("grp", "dev")), P(), split, P(("grp", "dev")), P(), P())
    return jax.shard_map(body, mesh=mesh, in_specs=in_specs, out_specs=(split, split), check_vma=False)
```
